32 devices in a mesh: grp: 16 (over z, y, core), mem: 2 (over x).
Axes of the slice: x: 2, y: 2, z: 4, core: 2. Of those that a mesh axis runs over, the one named last changes fastest.
Arguments:
- blocks: bfloat16 [384, 27, 128, 128], P(('grp', 'mem'))
- prolong: bfloat16 [384, 128, 128], P(('grp', 'mem'))
- cols: int32 [384, 27], P(('grp', 'mem')), may hold values from 0 to 11, as said below
- codes: int32 [384], P(('grp', 'mem')), may hold values from 1 to 15, as said below
Outputs:
- coarse_rows: bfloat16 [384, 27, 128, 128], P(('grp', 'mem'))
- diag_inverse: float32 [384, 128, 128], P('grp', 'mem')
The draws below stay inside these ranges and needn't reach their ends.
Inputs may be any that keep to these rules, and one draw needn't show every extreme that they name: codes is the same for the fine rows in slot s of partition m of every group, and the codes of one device's 12 rows are distinct, so the matching is symmetric and a device pairs with each other group at most once. Entry 13 of every row of cols is the row's own slot.
All inputs are finite; a program needn't handle non-finite values.
Results may differ from the reference program's by a relative error of at most 0.0036.
Values may be sent and summed in bfloat16 or wider, within the bound.
A program may use at most 128 MiB of HBM per device.

```python
import jax
import jax.numpy as jnp
from jax import lax

B = 128
K = 27
ROW_DEV = 12
NEWTON = 2
ROWS = 384
N_GRP = 16
N_MEM = 2


def draw_blocks(key, part):
    noise = jax.random.normal(key, (ROWS, K, B, B), jnp.float32) * (0.5 / B ** 0.5)
    center = (jnp.arange(K) == 13).astype(jnp.float32)
    diag_vals = jax.random.uniform(jax.random.fold_in(key, 7), (ROWS, 1, B, 1), jnp.float32, 2.0, 4.0)
    eye = jnp.eye(B, dtype=jnp.float32)
    return (noise + center[None, :, None, None] * eye[None, None] * diag_vals).astype(jnp.bfloat16)


def draw_prolong(key, part):
    noise = jax.random.normal(key, (ROWS, B, B), jnp.float32) * (0.3 / B ** 0.5)
    return (jnp.eye(B, dtype=jnp.float32)[None] + noise).astype(jnp.bfloat16)


def draw_cols(key, part):
    picks = jax.random.randint(key, (ROWS, K), 0, ROW_DEV).astype(jnp.int32)
    own_slot = (jnp.arange(ROWS, dtype=jnp.int32) % ROW_DEV)[:, None]
    center = (jnp.arange(K, dtype=jnp.int32) == 13)[None, :]
    return jnp.where(center, own_slot, picks).astype(jnp.int32)


def draw_codes(key, part):

    def one_member(member):
        order = jax.random.permutation(jax.random.fold_in(key, member), N_GRP - 1)
        return order[:ROW_DEV].astype(jnp.int32) + 1
    table = jax.vmap(one_member)(jnp.arange(N_MEM, dtype=jnp.int32))
    return jnp.broadcast_to(table[None], (N_GRP, N_MEM, ROW_DEV)).reshape(ROWS).astype(jnp.int32)


def setup_inputs(seed: int = 0) -> dict:
    streams_of = jax.random.split(jax.random.key(seed), 5)
    return {
        "blocks": draw_blocks(jax.random.fold_in(streams_of[4], 71), 0),
        "prolong": draw_prolong(jax.random.fold_in(streams_of[4], 71), 0),
        "cols": draw_cols(jax.random.fold_in(streams_of[4], 71), 0),
        "codes": draw_codes(jax.random.fold_in(streams_of[4], 71), 0),
    }


def newton_inverse(dmat):
    eye = jnp.eye(dmat.shape[0], dtype=jnp.float32)
    approx = eye * (1.0 / jnp.diagonal(dmat))[:, None]
    for step in range(NEWTON):
        inner = jnp.dot(dmat, approx, precision=lax.Precision.HIGHEST)
        approx = jnp.dot(approx, 2.0 * eye - inner, precision=lax.Precision.HIGHEST)
    return approx


def reference(blocks, prolong, cols, codes):
    rows = blocks.shape[0]
    index = jnp.arange(rows, dtype=jnp.int32)
    base = (index // ROW_DEV) * ROW_DEV
    global_cols = (base[:, None] + cols).astype(jnp.int32)
    span = N_MEM * ROW_DEV
    partner = ((index // span) ^ codes) * span + index % span

    def right_row(r):
        left_blocks = blocks[r].astype(jnp.float32)
        right_blocks = prolong[global_cols[r]].astype(jnp.float32)
        return jnp.einsum("kab,kbc->kac", left_blocks, right_blocks).astype(jnp.bfloat16)

    right = lax.map(right_row, index)

    def term_row(r):
        return jnp.einsum("ba,kbc->kac", prolong[r].astype(jnp.float32), right[r].astype(jnp.float32))

    def coarse_row(r):
        total = term_row(r) + term_row(partner[r])
        return total.astype(jnp.bfloat16), newton_inverse(total[13])

    coarse_rows, diag_inverse = lax.map(coarse_row, index)
    return coarse_rows, diag_inverse
```

```python
import functools

import jax
import jax.numpy as jnp
from jax import lax
from jax.experimental import pallas as pl
from jax.experimental.pallas import tpu as pltpu
from jax.sharding import PartitionSpec as P

NEWTON = 2
DIAG = 13
F32 = jnp.float32
BF16 = jnp.bfloat16
MESH = pl.DeviceIdType.MESH


def xor_peer(me, code, groups):
    out = 0
    bit = 1
    while bit < groups:
        mine = (me // bit) % 2
        theirs = (code // bit) % 2
        out = out + bit * (mine + theirs - 2 * mine * theirs)
        bit *= 2
    return out


def chunk_bounds(k):
    size = -(-k // 3)
    bounds = [(a, min(size, k - a)) for a in range(0, k, size)]
    first = [c for c in bounds if c[0] <= DIAG < c[0] + c[1]]
    return first + [c for c in bounds if c not in first]


def kernel(groups, mems, chunks, blocks_hbm, prolong, cols, codes, rows_hbm, inv_hbm, *scratch):
    nq = len(chunks)
    blk, send, low, recv = (scratch[i * nq:(i + 1) * nq] for i in range(4))
    (inverse, inv_all, load_sem, store_sem, send_sem, recv_sem, msend_sem, mrecv_sem, inv_sem) = scratch[4 * nq:]
    rows, width = prolong.shape[0], prolong.shape[1]
    share = width // mems
    me = lax.axis_index("grp")
    mem = lax.axis_index("mem")

    def load(q):
        a, size = chunks[q]
        return pltpu.make_async_copy(blocks_hbm.at[:, pl.ds(a, size)], blk[q], load_sem.at[q])

    for q in range(nq):
        load(q).start()

    barrier = pltpu.get_barrier_semaphore()
    for code in range(1, groups):
        pl.semaphore_signal(
            barrier, inc=1, device_id={"grp": xor_peer(me, code, groups)}, device_id_type=MESH)
    for off in range(1, mems):
        pl.semaphore_signal(
            barrier, inc=1, device_id={"mem": lax.rem(mem + off, mems)}, device_id_type=MESH)
    pl.semaphore_wait(barrier, groups - 1 + mems - 1)

    def remote(q, code):
        return pltpu.make_async_remote_copy(
            src_ref=send[q].at[code - 1],
            dst_ref=recv[q].at[code - 1],
            send_sem=send_sem.at[q, code - 1],
            recv_sem=recv_sem.at[q, code - 1],
            device_id={"grp": xor_peer(me, code, groups)},
            device_id_type=MESH,
        )

    half = groups // 2
    for q in range(nq):
        load(q).wait()
        a, size = chunks[q]

        def one_code(i, carry, q=q, a=a, size=size):
            code = groups - 1 - i // 2 - half * (i % 2)
            slot = 0
            for s in range(rows):
                slot = slot + jnp.where(codes[s] == code, s, 0)
            left = prolong[slot].T
            for kk in range(size):
                right = jnp.dot(
                    blk[q][slot, kk], prolong[cols[slot, a + kk]], preferred_element_type=F32
                ).astype(BF16)
                term = jnp.dot(left, right, preferred_element_type=F32)
                high = term.astype(BF16)
                send[q][code - 1, kk] = high
                low[q][code - 1, kk] = (term - high.astype(F32)).astype(BF16)
            remote(q, code).start()
            return carry

        lax.fori_loop(0, groups - 1, one_code, 0)

    def pair_block(q, place, kk):
        own = send[q][place, kk].astype(F32) + low[q][place, kk].astype(F32)
        return own + recv[q][place, kk].astype(F32)

    def place_of(s):
        return jnp.maximum(codes[s] - 1, 0)

    def store(q):
        a, size = chunks[q]
        return pltpu.make_async_copy(blk[q], rows_hbm.at[:, pl.ds(a, size)], store_sem.at[q])

    def inv_remote(off):
        to = lax.rem(mem + off, mems)
        return pltpu.make_async_remote_copy(
            src_ref=inverse.at[:, pl.ds(pl.multiple_of(to * share, share), share)],
            dst_ref=inv_all.at[mem],
            send_sem=msend_sem.at[off],
            recv_sem=mrecv_sem.at[off],
            device_id={"mem": to},
            device_id_type=MESH,
        )

    for q in range(nq):
        a, size = chunks[q]

        def arrived(i, carry, q=q):
            remote(q, i + 1).wait_recv()
            return carry

        lax.fori_loop(0, groups - 1, arrived, 0)

        def one_row(s, carry, q=q, size=size):
            place = place_of(s)
            for kk in range(size):
                blk[q][s, kk] = pair_block(q, place, kk).astype(BF16)
            return carry

        lax.fori_loop(0, rows, one_row, 0)
        store(q).start()

        if a <= DIAG < a + size:
            step = max(u for u in (1, 2, 3, 4) if rows % u == 0)
            eye = (lax.broadcasted_iota(jnp.int32, (width, width), 0)
                   == lax.broadcasted_iota(jnp.int32, (width, width), 1)).astype(F32)
            dot = functools.partial(jnp.dot, precision=lax.Precision.HIGHEST, preferred_element_type=F32)

            def some_inverses(j, carry, q=q, a=a):
                mats = [pair_block(q, place_of(j * step + u), DIAG - a) for u in range(step)]
                approx = [eye * (1.0 / jnp.sum(d * eye, axis=1, keepdims=True)) for d in mats]
                for _ in range(NEWTON):
                    inner = [dot(d, x) for d, x in zip(mats, approx)]
                    approx = [dot(x, 2.0 * eye - y) for x, y in zip(approx, inner)]
                for u in range(step):
                    inverse[j * step + u] = approx[u]
                return carry

            lax.fori_loop(0, rows // step, some_inverses, 0)
            for off in range(1, mems):
                inv_remote(off).start()
            mine = pltpu.make_async_copy(
                inverse.at[:, pl.ds(pl.multiple_of(mem * share, share), share)],
                inv_all.at[mem], inv_sem.at[0])
            mine.start()
            mine.wait()

    for off in range(1, mems):
        inv_remote(off).wait()
    out = pltpu.make_async_copy(inv_all, inv_hbm, inv_sem.at[1])
    out.start()
    for q in range(nq):
        def sent(i, carry, q=q):
            remote(q, i + 1).wait_send()
            return carry

        lax.fori_loop(0, groups - 1, sent, 0)
        store(q).wait()
    out.wait()


def local(groups, mems, blocks, prolong, cols, codes):
    rows, k, width, _ = blocks.shape
    chunks = chunk_bounds(k)
    nq = len(chunks)
    share = width // mems
    peers = groups - 1
    wide = [pltpu.VMEM((peers, size, width, width), BF16) for _, size in chunks]
    scratch = (
        [pltpu.VMEM((rows, size, width, width), BF16) for _, size in chunks]
        + wide + wide + wide
        + [
            pltpu.VMEM((rows, width, width), F32),
            pltpu.VMEM((mems, rows, share, width), F32),
            pltpu.SemaphoreType.DMA((nq,)),
            pltpu.SemaphoreType.DMA((nq,)),
            pltpu.SemaphoreType.DMA((nq, peers)),
            pltpu.SemaphoreType.DMA((nq, peers)),
            pltpu.SemaphoreType.DMA((mems,)),
            pltpu.SemaphoreType.DMA((mems,)),
            pltpu.SemaphoreType.DMA((2,)),
        ]
    )
    coarse, inverse = pl.pallas_call(
        functools.partial(kernel, groups, mems, chunks),
        out_shape=(
            jax.ShapeDtypeStruct(blocks.shape, BF16),
            jax.ShapeDtypeStruct((mems, rows, share, width), F32),
        ),
        in_specs=[
            pl.BlockSpec(memory_space=pl.ANY),
            pl.BlockSpec(memory_space=pltpu.VMEM),
            pl.BlockSpec(memory_space=pltpu.SMEM),
            pl.BlockSpec(memory_space=pltpu.SMEM),
        ],
        out_specs=(pl.BlockSpec(memory_space=pl.ANY), pl.BlockSpec(memory_space=pl.ANY)),
        scratch_shapes=scratch,
        compiler_params=pltpu.CompilerParams(
            collective_id=0, has_side_effects=True, vmem_limit_bytes=60 * 1024 * 1024),
        cost_estimate=pl.CostEstimate(
            flops=4 * rows * k * width ** 3, bytes_accessed=4 * rows * k * width * width, transcendentals=0),
        name="pair_terms",
    )(blocks, prolong, cols, codes)
    return coarse, inverse.reshape(mems * rows, share, width)


def solution(mesh):
    in_specs = (
        P(("grp", "mem"), None, None, None),
        P(("grp", "mem"), None, None),
        P(("grp", "mem"), None),
        P(("grp", "mem")),
    )
    out_specs = (P(("grp", "mem"), None, None, None), P("grp", "mem", None))
    return jax.shard_map(
        functools.partial(local, mesh.shape["grp"], mesh.shape["mem"]),
        mesh=mesh, in_specs=in_specs, out_specs=out_specs, check_vma=False)
```

```python
import functools

import jax
import jax.numpy as jnp
from jax import lax
from jax.experimental import pallas as pl
from jax.experimental.pallas import tpu as pltpu
from jax.sharding import PartitionSpec as P

NEWTON = 2
DIAG = 13
F32 = jnp.float32
BF16 = jnp.bfloat16
MESH = pl.DeviceIdType.MESH
WINDOW = 2


def xor_peer(me, code, groups):
    out = 0
    bit = 1
    while bit < groups:
        mine = (me // bit) % 2
        theirs = (code // bit) % 2
        out = out + bit * (mine + theirs - 2 * mine * theirs)
        bit *= 2
    return out


def chunk_bounds(k, size=4, near=1):
    start, end = max(DIAG - near, 0), min(DIAG + near + 1, k)
    bounds = [(start, end - start)]
    for low, high in ((0, start), (end, k)):
        bounds += [(a, min(size, high - a)) for a in range(low, high, size)]
    return bounds


def kernel(groups, mems, chunks, blocks_hbm, prolong, cols, codes, rows_hbm, inv_hbm, *scratch):
    nq = len(chunks)
    blk, send, low, recv = (scratch[i * nq:(i + 1) * nq] for i in range(4))
    (inverse, inv_all, load_sem, store_sem, send_sem, recv_sem, msend_sem, mrecv_sem, inv_sem) = scratch[4 * nq:]
    rows, width = prolong.shape[0], prolong.shape[1]
    share = width // mems
    me = lax.axis_index("grp")
    mem = lax.axis_index("mem")

    def load(q):
        a, size = chunks[q]
        return pltpu.make_async_copy(blocks_hbm.at[:, pl.ds(a, size)], blk[q], load_sem.at[q])

    for q in range(nq):
        load(q).start()

    barrier = pltpu.get_barrier_semaphore()
    for code in range(1, groups):
        pl.semaphore_signal(
            barrier, inc=1, device_id={"grp": xor_peer(me, code, groups)}, device_id_type=MESH)
    for off in range(1, mems):
        pl.semaphore_signal(
            barrier, inc=1, device_id={"mem": lax.rem(mem + off, mems)}, device_id_type=MESH)
    pl.semaphore_wait(barrier, groups - 1 + mems - 1)

    def remote(q, code):
        return pltpu.make_async_remote_copy(
            src_ref=send[q].at[code - 1],
            dst_ref=recv[q].at[code - 1],
            send_sem=send_sem.at[q, code - 1],
            recv_sem=recv_sem.at[q, code - 1],
            device_id={"grp": xor_peer(me, code, groups)},
            device_id_type=MESH,
        )

    half = groups // 2

    def send_chunk(q):
        load(q).wait()
        a, size = chunks[q]

        def one_code(i, carry):
            code = groups - 1 - i // 2 - half * (i % 2)
            slot = 0
            for s in range(rows):
                slot = slot + jnp.where(codes[s] == code, s, 0)
            left = prolong[slot].T
            for kk in range(size):
                right = jnp.dot(
                    blk[q][slot, kk], prolong[cols[slot, a + kk]], preferred_element_type=F32
                ).astype(BF16)
                term = jnp.dot(left, right, preferred_element_type=F32)
                high = term.astype(BF16)
                send[q][code - 1, kk] = high
                low[q][code - 1, kk] = (term - high.astype(F32)).astype(BF16)
            if q >= WINDOW:
                remote(q - WINDOW, code).wait_send()
            remote(q, code).start()
            return carry

        lax.fori_loop(0, groups - 1, one_code, 0)

    def pair_block(q, place, kk):
        own = send[q][place, kk].astype(F32) + low[q][place, kk].astype(F32)
        return own + recv[q][place, kk].astype(F32)

    def place_of(s):
        return jnp.maximum(codes[s] - 1, 0)

    def store(q):
        a, size = chunks[q]
        return pltpu.make_async_copy(blk[q], rows_hbm.at[:, pl.ds(a, size)], store_sem.at[q])

    def inv_remote(off):
        to = lax.rem(mem + off, mems)
        return pltpu.make_async_remote_copy(
            src_ref=inverse.at[:, pl.ds(pl.multiple_of(to * share, share), share)],
            dst_ref=inv_all.at[mem],
            send_sem=msend_sem.at[off],
            recv_sem=mrecv_sem.at[off],
            device_id={"mem": to},
            device_id_type=MESH,
        )

    def inverses(q):
        step = max(u for u in (1, 2, 3, 4) if rows % u == 0)
        eye = (lax.broadcasted_iota(jnp.int32, (width, width), 0)
               == lax.broadcasted_iota(jnp.int32, (width, width), 1)).astype(F32)
        dot = functools.partial(jnp.dot, precision=lax.Precision.HIGHEST, preferred_element_type=F32)

        def some_inverses(j, carry):
            mats = [pair_block(q, place_of(j * step + u), DIAG - chunks[q][0]) for u in range(step)]
            approx = [eye * (1.0 / jnp.sum(d * eye, axis=1, keepdims=True)) for d in mats]
            for _ in range(NEWTON):
                inner = [dot(d, x) for d, x in zip(mats, approx)]
                approx = [dot(x, 2.0 * eye - y) for x, y in zip(approx, inner)]
            for u in range(step):
                inverse[j * step + u] = approx[u]
            return carry

        lax.fori_loop(0, rows // step, some_inverses, 0)
        for off in range(1, mems):
            inv_remote(off).start()
        mine = pltpu.make_async_copy(
            inverse.at[:, pl.ds(pl.multiple_of(mem * share, share), share)],
            inv_all.at[mem], inv_sem.at[0])
        mine.start()
        mine.wait()

    def sum_chunk(q):
        def arrived(i, carry):
            remote(q, i + 1).wait_recv()
            return carry

        lax.fori_loop(0, groups - 1, arrived, 0)

        def one_row(s, carry):
            place = place_of(s)
            for kk in range(chunks[q][1]):
                blk[q][s, kk] = pair_block(q, place, kk).astype(BF16)
            return carry

        lax.fori_loop(0, rows, one_row, 0)
        store(q).start()
        if chunks[q][0] <= DIAG < chunks[q][0] + chunks[q][1]:
            inverses(q)

    for q in range(nq + WINDOW):
        if q < nq:
            send_chunk(q)
        if q >= WINDOW:
            sum_chunk(q - WINDOW)

    for off in range(1, mems):
        inv_remote(off).wait()
    out = pltpu.make_async_copy(inv_all, inv_hbm, inv_sem.at[1])
    out.start()
    for q in range(max(nq - WINDOW, 0), nq):
        def sent(i, carry, q=q):
            remote(q, i + 1).wait_send()
            return carry

        lax.fori_loop(0, groups - 1, sent, 0)
    for q in range(nq):
        store(q).wait()
    out.wait()


def local(groups, mems, blocks, prolong, cols, codes):
    rows, k, width, _ = blocks.shape
    chunks = chunk_bounds(k)
    nq = len(chunks)
    share = width // mems
    peers = groups - 1
    wide = [pltpu.VMEM((peers, size, width, width), BF16) for _, size in chunks]
    scratch = (
        [pltpu.VMEM((rows, size, width, width), BF16) for _, size in chunks]
        + wide + wide + wide
        + [
            pltpu.VMEM((rows, width, width), F32),
            pltpu.VMEM((mems, rows, share, width), F32),
            pltpu.SemaphoreType.DMA((nq,)),
            pltpu.SemaphoreType.DMA((nq,)),
            pltpu.SemaphoreType.DMA((nq, peers)),
            pltpu.SemaphoreType.DMA((nq, peers)),
            pltpu.SemaphoreType.DMA((mems,)),
            pltpu.SemaphoreType.DMA((mems,)),
            pltpu.SemaphoreType.DMA((2,)),
        ]
    )
    coarse, inverse = pl.pallas_call(
        functools.partial(kernel, groups, mems, chunks),
        out_shape=(
            jax.ShapeDtypeStruct(blocks.shape, BF16),
            jax.ShapeDtypeStruct((mems, rows, share, width), F32),
        ),
        in_specs=[
            pl.BlockSpec(memory_space=pl.ANY),
            pl.BlockSpec(memory_space=pltpu.VMEM),
            pl.BlockSpec(memory_space=pltpu.SMEM),
            pl.BlockSpec(memory_space=pltpu.SMEM),
        ],
        out_specs=(pl.BlockSpec(memory_space=pl.ANY), pl.BlockSpec(memory_space=pl.ANY)),
        scratch_shapes=scratch,
        compiler_params=pltpu.CompilerParams(
            collective_id=0, has_side_effects=True, vmem_limit_bytes=60 * 1024 * 1024),
        cost_estimate=pl.CostEstimate(
            flops=4 * rows * k * width ** 3, bytes_accessed=4 * rows * k * width * width, transcendentals=0),
        name="pair_terms",
    )(blocks, prolong, cols, codes)
    return coarse, inverse.reshape(mems * rows, share, width)


def solution(mesh):
    in_specs = (
        P(("grp", "mem"), None, None, None),
        P(("grp", "mem"), None, None),
        P(("grp", "mem"), None),
        P(("grp", "mem")),
    )
    out_specs = (P(("grp", "mem"), None, None, None), P("grp", "mem", None))
    return jax.shard_map(
        functools.partial(local, mesh.shape["grp"], mesh.shape["mem"]),
        mesh=mesh, in_specs=in_specs, out_specs=out_specs, check_vma=False)
```

```python
import functools

import jax
import jax.numpy as jnp
from jax import lax
from jax.experimental import pallas as pl
from jax.experimental.pallas import tpu as pltpu
from jax.sharding import PartitionSpec as P

NEWTON = 2
DIAG = 13
F32 = jnp.float32
BF16 = jnp.bfloat16
MESH = pl.DeviceIdType.MESH
WINDOW = 2
MAX_DROP = 2


def xor_peer(me, code, groups):
    out = 0
    bit = 1
    while bit < groups:
        mine = (me // bit) % 2
        theirs = (code // bit) % 2
        out = out + bit * (mine + theirs - 2 * mine * theirs)
        bit *= 2
    return out


def chunk_bounds(k, size=4):
    start, end = max(DIAG - 1, 0), min(DIAG + 2, k)
    bounds = [(DIAG, 1)] + [(a, 1) for a in range(start, end) if a != DIAG]
    for low, high in ((0, start), (end, k)):
        bounds += [(a, min(size, high - a)) for a in range(low, high, size)]
    return bounds


def kernel(groups, mems, chunks, drop, blocks_hbm, prolong, cols, codes, rows_hbm, inv_hbm, *scratch):
    nq = len(chunks)
    blk, send, low, recv = (scratch[i * nq:(i + 1) * nq] for i in range(4))
    hop = scratch[4 * nq:5 * nq] if drop else None
    (inverse, inv_all, load_sem, store_sem, send_sem, recv_sem, msend_sem, mrecv_sem, inv_sem,
     *hop_sems) = scratch[(5 if drop else 4) * nq:]
    half = groups // 2
    kept = groups - 1 - drop
    stages = (groups - 1).bit_length() - 1
    rows, width = prolong.shape[0], prolong.shape[1]
    share = width // mems
    me = lax.axis_index("grp")
    mem = lax.axis_index("mem")

    def load(q):
        a, size = chunks[q]
        return pltpu.make_async_copy(blocks_hbm.at[:, pl.ds(a, size)], blk[q], load_sem.at[q])

    for q in range(nq):
        load(q).start()

    barrier = pltpu.get_barrier_semaphore()
    for code in range(1, groups):
        pl.semaphore_signal(
            barrier, inc=1, device_id={"grp": xor_peer(me, code, groups)}, device_id_type=MESH)
    for off in range(1, mems):
        pl.semaphore_signal(
            barrier, inc=1, device_id={"mem": lax.rem(mem + off, mems)}, device_id_type=MESH)
    pl.semaphore_wait(barrier, groups - 1 + mems - 1)

    def remote(q, code):
        return pltpu.make_async_remote_copy(
            src_ref=send[q].at[code - 1],
            dst_ref=recv[q].at[code - 1],
            send_sem=send_sem.at[q, code - 1],
            recv_sem=recv_sem.at[q, code - 1],
            device_id={"grp": xor_peer(me, code, groups)},
            device_id_type=MESH,
        )

    dropped = [groups - 1 - i for i in range(drop)]
    riding = [jnp.int32(0)] * drop
    if drop:
        taken = {}
        for c in range(half, groups):
            taken[c] = sum(jnp.where(codes[s] == c, 1, 0) for s in range(rows))
        rank, count = [], jnp.int32(0)
        for c in dropped:
            rank.append(count)
            count = count + taken[c]
        free = jnp.int32(0)
        for c in range(half, kept + 1):
            for i, d in enumerate(dropped):
                fits = jnp.logical_and(
                    jnp.logical_and(taken[c] == 0, taken[d] == 1), free == rank[i])
                riding[i] = jnp.where(fits, c, riding[i])
            free = free + (1 - taken[c])

    def slot_of(code):
        slot = 0
        for s in range(rows):
            slot = slot + jnp.where(codes[s] == code, s, 0)
        return slot

    def make_terms(q, code):
        a, size = chunks[q]
        slot = slot_of(code)
        left = prolong[slot].T
        for kk in range(size):
            right = jnp.dot(
                blk[q][slot, kk], prolong[cols[slot, a + kk]], preferred_element_type=F32
            ).astype(BF16)
            term = jnp.dot(left, right, preferred_element_type=F32)
            high = term.astype(BF16)
            low[q][code - 1, kk] = (term - high.astype(F32)).astype(BF16)
            if drop and not isinstance(code, int):
                for i in range(drop):
                    high = jnp.where(code == riding[i], hop[q][stages - 2, i, kk], high)
            send[q][code - 1, kk] = high

    def held(q, stage, i):
        if stage == 0:
            return send[q].at[dropped[i] - 1]
        if stage == 1:
            return recv[q].at[dropped[i] - 1]
        return hop[q].at[stage - 2, i]

    def exchange(q, stage, i):
        return pltpu.make_async_remote_copy(
            src_ref=held(q, stage, i),
            dst_ref=held(q, stage + 1, i),
            send_sem=hop_sems[0].at[q, stage, i],
            recv_sem=hop_sems[1].at[q, stage, i],
            device_id={"grp": xor_peer(me, 2 ** stage, groups)},
            device_id_type=MESH,
        )

    def hops_at(time):
        if not drop:
            return []
        return [(time + stages - b, b) for b in range(stages) if 0 <= time + stages - b < nq]

    def start_hops(time):
        for q, b in reversed(hops_at(time)):
            if b == 0:
                load(q).wait()
                for code in dropped:
                    make_terms(q, code)
            for i in range(drop):
                exchange(q, b, i).start()

    def finish_hops(time):
        for q, b in reversed(hops_at(time)):
            for i in range(drop):
                exchange(q, b, i).wait()
                ride = jnp.where(riding[i] == 0, dropped[i], riding[i])
                moves = (ride // 2 ** b) % 2 != (dropped[i] // 2 ** b) % 2
                before, after = held(q, b, i), held(q, b + 1, i)
                for kk in range(chunks[q][1]):
                    after[kk] = jnp.where(moves, after[kk], before[kk])

    def send_chunk(q):
        if not drop:
            load(q).wait()

        def one_code(i, carry):
            if half - drop >= half - 1:
                code = kept - i // 2 - (half - drop) * (i % 2)
            else:
                code = half - 1 - i // 2 + (half - drop) * (i % 2)
            make_terms(q, code)
            if q >= WINDOW:
                remote(q - WINDOW, code).wait_send()
            remote(q, code).start()
            return carry

        lax.fori_loop(0, kept, one_code, 0)

    def pair_block(q, place, kk):
        mine, theirs = place
        own = send[q][mine, kk].astype(F32) + low[q][mine, kk].astype(F32)
        return own + recv[q][theirs, kk].astype(F32)

    def place_of(s):
        mine = codes[s]
        theirs = mine
        for i in range(drop):
            theirs = jnp.where(mine == dropped[i], riding[i], theirs)
        return jnp.maximum(mine - 1, 0), jnp.maximum(theirs - 1, 0)

    def store(q):
        a, size = chunks[q]
        return pltpu.make_async_copy(blk[q], rows_hbm.at[:, pl.ds(a, size)], store_sem.at[q])

    def inv_remote(off):
        to = lax.rem(mem + off, mems)
        return pltpu.make_async_remote_copy(
            src_ref=inverse.at[:, pl.ds(pl.multiple_of(to * share, share), share)],
            dst_ref=inv_all.at[mem],
            send_sem=msend_sem.at[off],
            recv_sem=mrecv_sem.at[off],
            device_id={"mem": to},
            device_id_type=MESH,
        )

    def inverses(q):
        step = max(u for u in (1, 2, 3, 4) if rows % u == 0)
        eye = (lax.broadcasted_iota(jnp.int32, (width, width), 0)
               == lax.broadcasted_iota(jnp.int32, (width, width), 1)).astype(F32)
        dot = functools.partial(jnp.dot, precision=lax.Precision.HIGHEST, preferred_element_type=F32)

        def some_inverses(j, carry):
            mats = [pair_block(q, place_of(j * step + u), DIAG - chunks[q][0]) for u in range(step)]
            approx = [eye * (1.0 / jnp.sum(d * eye, axis=1, keepdims=True)) for d in mats]
            for _ in range(NEWTON):
                inner = [dot(d, x) for d, x in zip(mats, approx)]
                approx = [dot(x, 2.0 * eye - y) for x, y in zip(approx, inner)]
            for u in range(step):
                inverse[j * step + u] = approx[u]
            return carry

        lax.fori_loop(0, rows // step, some_inverses, 0)
        for off in range(1, mems):
            inv_remote(off).start()
        mine = pltpu.make_async_copy(
            inverse.at[:, pl.ds(pl.multiple_of(mem * share, share), share)],
            inv_all.at[mem], inv_sem.at[0])
        mine.start()
        mine.wait()

    def sum_chunk(q):
        def arrived(i, carry):
            remote(q, i + 1).wait_recv()
            return carry

        lax.fori_loop(0, kept, arrived, 0)

        def one_row(s, carry):
            place = place_of(s)
            for kk in range(chunks[q][1]):
                blk[q][s, kk] = pair_block(q, place, kk).astype(BF16)
            return carry

        lax.fori_loop(0, rows, one_row, 0)
        store(q).start()
        if chunks[q][0] <= DIAG < chunks[q][0] + chunks[q][1]:
            inverses(q)

    for time in range(-stages, 0):
        start_hops(time)
        finish_hops(time)
    for q in range(nq + WINDOW):
        if q < nq:
            start_hops(q)
            send_chunk(q)
        if q >= WINDOW:
            sum_chunk(q - WINDOW)
        if q < nq:
            finish_hops(q)

    for off in range(1, mems):
        inv_remote(off).wait()
    out = pltpu.make_async_copy(inv_all, inv_hbm, inv_sem.at[1])
    out.start()
    for q in range(max(nq - WINDOW, 0), nq):
        def sent(i, carry, q=q):
            remote(q, i + 1).wait_send()
            return carry

        lax.fori_loop(0, kept, sent, 0)
    for q in range(nq):
        store(q).wait()
    out.wait()


def pair_terms(groups, mems, drop, blocks, prolong, cols, codes):
    rows, k, width, _ = blocks.shape
    chunks = chunk_bounds(k)
    nq = len(chunks)
    share = width // mems
    peers = groups - 1
    stages = peers.bit_length() - 1
    wide = [pltpu.VMEM((peers, size, width, width), BF16) for _, size in chunks]
    scratch = (
        [pltpu.VMEM((rows, size, width, width), BF16) for _, size in chunks]
        + wide + wide + wide
        + ([pltpu.VMEM((stages - 1, drop, size, width, width), BF16) for _, size in chunks] if drop else [])
        + [
            pltpu.VMEM((rows, width, width), F32),
            pltpu.VMEM((mems, rows, share, width), F32),
            pltpu.SemaphoreType.DMA((nq,)),
            pltpu.SemaphoreType.DMA((nq,)),
            pltpu.SemaphoreType.DMA((nq, peers)),
            pltpu.SemaphoreType.DMA((nq, peers)),
            pltpu.SemaphoreType.DMA((mems,)),
            pltpu.SemaphoreType.DMA((mems,)),
            pltpu.SemaphoreType.DMA((2,)),
        ]
        + ([pltpu.SemaphoreType.DMA((nq, stages, drop))] * 2 if drop else [])
    )
    coarse, inverse = pl.pallas_call(
        functools.partial(kernel, groups, mems, chunks, drop),
        out_shape=(
            jax.ShapeDtypeStruct(blocks.shape, BF16),
            jax.ShapeDtypeStruct((mems, rows, share, width), F32),
        ),
        in_specs=[
            pl.BlockSpec(memory_space=pl.ANY),
            pl.BlockSpec(memory_space=pltpu.VMEM),
            pl.BlockSpec(memory_space=pltpu.SMEM),
            pl.BlockSpec(memory_space=pltpu.SMEM),
        ],
        out_specs=(pl.BlockSpec(memory_space=pl.ANY), pl.BlockSpec(memory_space=pl.ANY)),
        scratch_shapes=scratch,
        compiler_params=pltpu.CompilerParams(
            collective_id=drop, has_side_effects=True, vmem_limit_bytes=62 * 1024 * 1024),
        cost_estimate=pl.CostEstimate(
            flops=4 * rows * k * width ** 3, bytes_accessed=4 * rows * k * width * width, transcendentals=0),
        name="pair_terms_%d" % drop,
    )(blocks, prolong, cols, codes)
    return coarse, inverse.reshape(mems * rows, share, width)


def local(groups, mems, blocks, prolong, cols, codes):
    half = groups // 2
    absent = half - jnp.sum((codes >= half).astype(jnp.int32))
    drop = jnp.clip(lax.pmin(absent, "mem"), 0, MAX_DROP)
    branches = [functools.partial(pair_terms, groups, mems, d) for d in range(MAX_DROP + 1)]
    return lax.switch(drop, branches, blocks, prolong, cols, codes)


def solution(mesh):
    in_specs = (
        P(("grp", "mem"), None, None, None),
        P(("grp", "mem"), None, None),
        P(("grp", "mem"), None),
        P(("grp", "mem")),
    )
    out_specs = (P(("grp", "mem"), None, None, None), P("grp", "mem", None))
    return jax.shard_map(
        functools.partial(local, mesh.shape["grp"], mesh.shape["mem"]),
        mesh=mesh, in_specs=in_specs, out_specs=out_specs, check_vma=False)
```

```python
import functools

import jax
import jax.numpy as jnp
from jax import lax
from jax.experimental import pallas as pl
from jax.experimental.pallas import tpu as pltpu
from jax.sharding import PartitionSpec as P

NEWTON = 2
DIAG = 13
F32 = jnp.float32
BF16 = jnp.bfloat16
MESH = pl.DeviceIdType.MESH
WINDOW = 2
MAX_DROP = 2


def xor_peer(me, code, groups):
    out = 0
    bit = 1
    while bit < groups:
        mine = (me // bit) % 2
        theirs = (code // bit) % 2
        out = out + bit * (mine + theirs - 2 * mine * theirs)
        bit *= 2
    return out


def chunk_bounds(k, size=4, tail=2):
    start, end = max(DIAG - 1, 0), min(DIAG + 2, k)
    bounds = [(DIAG, 1)] + [(a, 1) for a in range(start, end) if a != DIAG]
    for low, high in ((0, start), (end, k)):
        bounds += [(a, min(size, high - a)) for a in range(low, high, size)]
    a, last = bounds[-1]
    if last > tail:
        bounds[-1:] = [(a, last - tail), (a + last - tail, tail)]
    return bounds


def kernel(groups, mems, chunks, drop, blocks_hbm, prolong, cols, codes, rows_hbm, inv_hbm, *scratch):
    nq = len(chunks)
    blk, send, low, recv = (scratch[i * nq:(i + 1) * nq] for i in range(4))
    hop = scratch[4 * nq:5 * nq] if drop else None
    (inverse, inv_all, load_sem, store_sem, send_sem, recv_sem, msend_sem, mrecv_sem, inv_sem,
     *hop_sems) = scratch[(5 if drop else 4) * nq:]
    half = groups // 2
    kept = groups - 1 - drop
    stages = (groups - 1).bit_length() - 1
    rows, width = prolong.shape[0], prolong.shape[1]
    share = width // mems
    me = lax.axis_index("grp")
    mem = lax.axis_index("mem")

    def load(q):
        a, size = chunks[q]
        return pltpu.make_async_copy(blocks_hbm.at[:, pl.ds(a, size)], blk[q], load_sem.at[q])

    for q in range(nq):
        load(q).start()

    barrier = pltpu.get_barrier_semaphore()
    for code in range(1, groups):
        pl.semaphore_signal(
            barrier, inc=1, device_id={"grp": xor_peer(me, code, groups)}, device_id_type=MESH)
    for off in range(1, mems):
        pl.semaphore_signal(
            barrier, inc=1, device_id={"mem": lax.rem(mem + off, mems)}, device_id_type=MESH)
    pl.semaphore_wait(barrier, groups - 1 + mems - 1)

    def remote(q, code):
        return pltpu.make_async_remote_copy(
            src_ref=send[q].at[code - 1],
            dst_ref=recv[q].at[code - 1],
            send_sem=send_sem.at[q, code - 1],
            recv_sem=recv_sem.at[q, code - 1],
            device_id={"grp": xor_peer(me, code, groups)},
            device_id_type=MESH,
        )

    dropped = [groups - 1 - i for i in range(drop)]
    riding = [jnp.int32(0)] * drop
    if drop:
        taken = {}
        for c in range(half, groups):
            taken[c] = sum(jnp.where(codes[s] == c, 1, 0) for s in range(rows))
        rank, count = [], jnp.int32(0)
        for c in dropped:
            rank.append(count)
            count = count + taken[c]
        free = jnp.int32(0)
        for c in range(half, kept + 1):
            for i, d in enumerate(dropped):
                fits = jnp.logical_and(
                    jnp.logical_and(taken[c] == 0, taken[d] == 1), free == rank[i])
                riding[i] = jnp.where(fits, c, riding[i])
            free = free + (1 - taken[c])

    def slot_of(code):
        slot = 0
        for s in range(rows):
            slot = slot + jnp.where(codes[s] == code, s, 0)
        return slot

    def make_terms(q, code):
        a, size = chunks[q]
        slot = slot_of(code)
        left = prolong[slot].T
        for kk in range(size):
            right = jnp.dot(
                blk[q][slot, kk], prolong[cols[slot, a + kk]], preferred_element_type=F32
            ).astype(BF16)
            term = jnp.dot(left, right, preferred_element_type=F32)
            high = term.astype(BF16)
            low[q][code - 1, kk] = (term - high.astype(F32)).astype(BF16)
            if drop and q > 0 and not isinstance(code, int):
                for i in range(drop):
                    high = jnp.where(code == riding[i], hop[q][stages - 2, i, kk], high)
            send[q][code - 1, kk] = high

    def held(q, stage, i):
        if stage == 0:
            return send[q].at[dropped[i] - 1]
        if stage == 1:
            return recv[q].at[dropped[i] - 1]
        return hop[q].at[stage - 2, i]

    def exchange(q, stage, i):
        return pltpu.make_async_remote_copy(
            src_ref=held(q, stage, i),
            dst_ref=held(q, stage + 1, i),
            send_sem=hop_sems[0].at[q, stage, i],
            recv_sem=hop_sems[1].at[q, stage, i],
            device_id={"grp": xor_peer(me, 2 ** stage, groups)},
            device_id_type=MESH,
        )

    def hops_at(time):
        if not drop:
            return []
        return [(time + stages - b, b) for b in range(stages) if 1 <= time + stages - b < nq]

    def slots(q):
        return groups - 1 if q == 0 else kept

    def start_hops(time):
        for q, b in reversed(hops_at(time)):
            if b == 0:
                load(q).wait()
                for code in dropped:
                    make_terms(q, code)
            for i in range(drop):
                exchange(q, b, i).start()

    def finish_hops(time):
        for q, b in reversed(hops_at(time)):
            for i in range(drop):
                exchange(q, b, i).wait()
                ride = jnp.where(riding[i] == 0, dropped[i], riding[i])
                moves = (ride // 2 ** b) % 2 != (dropped[i] // 2 ** b) % 2
                before, after = held(q, b, i), held(q, b + 1, i)
                for kk in range(chunks[q][1]):
                    after[kk] = jnp.where(moves, after[kk], before[kk])

    def send_chunk(q):
        if not drop or q == 0:
            load(q).wait()
        spare = 0 if q == 0 else drop

        def one_code(i, carry):
            if half - spare >= half - 1:
                code = slots(q) - i // 2 - (half - spare) * (i % 2)
            else:
                code = half - 1 - i // 2 + (half - spare) * (i % 2)
            make_terms(q, code)
            if q >= WINDOW:
                remote(q - WINDOW, code).wait_send()
            remote(q, code).start()
            return carry

        lax.fori_loop(0, slots(q), one_code, 0)
        if q == WINDOW:
            for code in dropped:
                remote(0, code).wait_send()

    def pair_block(q, place, kk):
        mine, theirs = place
        own = send[q][mine, kk].astype(F32) + low[q][mine, kk].astype(F32)
        return own + recv[q][theirs, kk].astype(F32)

    def place_of(q, s):
        mine = codes[s]
        theirs = mine
        for i in range(drop if q > 0 else 0):
            theirs = jnp.where(mine == dropped[i], riding[i], theirs)
        return jnp.maximum(mine - 1, 0), jnp.maximum(theirs - 1, 0)

    def store(q):
        a, size = chunks[q]
        return pltpu.make_async_copy(blk[q], rows_hbm.at[:, pl.ds(a, size)], store_sem.at[q])

    def inv_remote(off):
        to = lax.rem(mem + off, mems)
        return pltpu.make_async_remote_copy(
            src_ref=inverse.at[:, pl.ds(pl.multiple_of(to * share, share), share)],
            dst_ref=inv_all.at[mem],
            send_sem=msend_sem.at[off],
            recv_sem=mrecv_sem.at[off],
            device_id={"mem": to},
            device_id_type=MESH,
        )

    def inverses(q):
        step = max(u for u in (1, 2, 3, 4) if rows % u == 0)
        eye = (lax.broadcasted_iota(jnp.int32, (width, width), 0)
               == lax.broadcasted_iota(jnp.int32, (width, width), 1)).astype(F32)
        dot = functools.partial(jnp.dot, precision=lax.Precision.HIGHEST, preferred_element_type=F32)

        def some_inverses(j, carry):
            mats = [pair_block(q, place_of(q, j * step + u), DIAG - chunks[q][0]) for u in range(step)]
            approx = [eye * (1.0 / jnp.sum(d * eye, axis=1, keepdims=True)) for d in mats]
            for _ in range(NEWTON):
                inner = [dot(d, x) for d, x in zip(mats, approx)]
                approx = [dot(x, 2.0 * eye - y) for x, y in zip(approx, inner)]
            for u in range(step):
                inverse[j * step + u] = approx[u]
            return carry

        lax.fori_loop(0, rows // step, some_inverses, 0)
        for off in range(1, mems):
            inv_remote(off).start()
        mine = pltpu.make_async_copy(
            inverse.at[:, pl.ds(pl.multiple_of(mem * share, share), share)],
            inv_all.at[mem], inv_sem.at[0])
        mine.start()
        mine.wait()

    def sum_chunk(q):
        def arrived(i, carry):
            remote(q, i + 1).wait_recv()
            return carry

        lax.fori_loop(0, slots(q), arrived, 0)

        def one_row(s, carry):
            place = place_of(q, s)
            for kk in range(chunks[q][1]):
                blk[q][s, kk] = pair_block(q, place, kk).astype(BF16)
            return carry

        lax.fori_loop(0, rows, one_row, 0)
        store(q).start()
        if chunks[q][0] <= DIAG < chunks[q][0] + chunks[q][1]:
            inverses(q)

    for time in range(1 - stages, 1):
        start_hops(time)
        if time == 1 - stages:
            send_chunk(0)
        finish_hops(time)
    for q in range(1, nq + WINDOW):
        if q < nq:
            start_hops(q)
            send_chunk(q)
        if q >= WINDOW:
            sum_chunk(q - WINDOW)
        if q < nq:
            finish_hops(q)

    for off in range(1, mems):
        inv_remote(off).wait()
    out = pltpu.make_async_copy(inv_all, inv_hbm, inv_sem.at[1])
    out.start()
    for q in range(max(nq - WINDOW, 0), nq):
        def sent(i, carry, q=q):
            remote(q, i + 1).wait_send()
            return carry

        lax.fori_loop(0, slots(q), sent, 0)
    for q in range(nq):
        store(q).wait()
    out.wait()


def pair_terms(groups, mems, drop, blocks, prolong, cols, codes):
    rows, k, width, _ = blocks.shape
    chunks = chunk_bounds(k)
    nq = len(chunks)
    share = width // mems
    peers = groups - 1
    stages = peers.bit_length() - 1
    wide = [pltpu.VMEM((peers, size, width, width), BF16) for _, size in chunks]
    scratch = (
        [pltpu.VMEM((rows, size, width, width), BF16) for _, size in chunks]
        + wide + wide + wide
        + ([pltpu.VMEM((stages - 1, drop, size, width, width), BF16) for _, size in chunks] if drop else [])
        + [
            pltpu.VMEM((rows, width, width), F32),
            pltpu.VMEM((mems, rows, share, width), F32),
            pltpu.SemaphoreType.DMA((nq,)),
            pltpu.SemaphoreType.DMA((nq,)),
            pltpu.SemaphoreType.DMA((nq, peers)),
            pltpu.SemaphoreType.DMA((nq, peers)),
            pltpu.SemaphoreType.DMA((mems,)),
            pltpu.SemaphoreType.DMA((mems,)),
            pltpu.SemaphoreType.DMA((2,)),
        ]
        + ([pltpu.SemaphoreType.DMA((nq, stages, drop))] * 2 if drop else [])
    )
    coarse, inverse = pl.pallas_call(
        functools.partial(kernel, groups, mems, chunks, drop),
        out_shape=(
            jax.ShapeDtypeStruct(blocks.shape, BF16),
            jax.ShapeDtypeStruct((mems, rows, share, width), F32),
        ),
        in_specs=[
            pl.BlockSpec(memory_space=pl.ANY),
            pl.BlockSpec(memory_space=pltpu.VMEM),
            pl.BlockSpec(memory_space=pltpu.SMEM),
            pl.BlockSpec(memory_space=pltpu.SMEM),
        ],
        out_specs=(pl.BlockSpec(memory_space=pl.ANY), pl.BlockSpec(memory_space=pl.ANY)),
        scratch_shapes=scratch,
        compiler_params=pltpu.CompilerParams(
            collective_id=drop, has_side_effects=True, vmem_limit_bytes=62 * 1024 * 1024),
        cost_estimate=pl.CostEstimate(
            flops=4 * rows * k * width ** 3, bytes_accessed=4 * rows * k * width * width, transcendentals=0),
        name="pair_terms_%d" % drop,
    )(blocks, prolong, cols, codes)
    return coarse, inverse.reshape(mems * rows, share, width)


def hand_over(src, dst, sem):
    copies = [pltpu.make_async_copy(src.at[r], dst.at[r], sem.at[r]) for r in range(src.shape[0])]
    for copy in copies:
        copy.start()
    for copy in copies:
        copy.wait()


def local(groups, mems, blocks, prolong, cols, codes):
    half = groups // 2
    absent = half - jnp.sum((codes >= half).astype(jnp.int32))
    drop = jnp.clip(lax.pmin(absent, "mem"), 0, MAX_DROP)
    branches = [functools.partial(pair_terms, groups, mems, d) for d in range(MAX_DROP + 1)]
    coarse, inverse = lax.switch(drop, branches, blocks, prolong, cols, codes)
    coarse = pl.pallas_call(
        hand_over,
        out_shape=jax.ShapeDtypeStruct(coarse.shape, coarse.dtype),
        in_specs=[pl.BlockSpec(memory_space=pl.ANY)],
        out_specs=pl.BlockSpec(memory_space=pl.ANY),
        scratch_shapes=[pltpu.SemaphoreType.DMA((coarse.shape[0],))],
        compiler_params=pltpu.CompilerParams(vmem_limit_bytes=62 * 1024 * 1024),
        name="hand_over",
    )(coarse)
    return coarse, inverse


def solution(mesh):
    in_specs = (
        P(("grp", "mem"), None, None, None),
        P(("grp", "mem"), None, None),
        P(("grp", "mem"), None),
        P(("grp", "mem")),
    )
    out_specs = (P(("grp", "mem"), None, None, None), P("grp", "mem", None))
    return jax.shard_map(
        functools.partial(local, mesh.shape["grp"], mesh.shape["mem"]),
        mesh=mesh, in_specs=in_specs, out_specs=out_specs, check_vma=False)
```
